32 devices in a mesh: rep: 2 (over y), tp: 16 (over z, x, core).
Axes of the slice: x: 2, y: 2, z: 4, core: 2. Of those that a mesh axis runs over, the one named last changes fastest.
Arguments:
- hidden: bfloat16 [64, 28672], P('rep', 'tp'), parts along dimension 0, may hold values from -6 to 6
- down_weight: bfloat16 [28672, 8192], P('tp'), may hold values from -0.03125 to 0.03125
- shrink_factor: bfloat16 [16, 64, 28672], P('tp'), may hold values from -0.03125 to 0.03125
- expand_factor: bfloat16 [16, 64, 8192], P('tp'), may hold values from -0.75 to 0.75
- variant_ids: int32 [64, 1], P('rep'), parts along dimension 0, may hold values from 0 to 15; in each aligned block of 32 rows (0 to 31, 32 to 63, ...) at most 8 rows name the same one
- owner: int32 [16], replicated, may hold values from 0 to 15, each once
Outputs:
- mixed: bfloat16 [64, 8192], P(('rep', 'tp')), parts along dimension 0
The draws below stay inside these ranges and needn't reach their ends.
There are 2 independent parts, one for each index of `rep`. The reference program is written for one: setup_inputs(seed, part) draws one part's arguments, and reference() takes and returns one part's arrays. A program takes and returns all parts, laid end to end along the dimension named above; an argument that names none is the same for every part. Nothing has to cross between parts.
Inputs may be any that keep to these rules, and one draw needn't show every extreme that they name: `variant_ids`: every variant is named by at least one request and by at most 8; some variant by exactly 8. `owner`: each slot holds exactly one variant.
All inputs are finite; a program needn't handle non-finite values.
Results may differ from the reference program's by a relative error of at most 0.005.
Values may be sent and summed in bfloat16 or wider, within the bound.
A program may use at most 128 MiB of HBM per device.

```python
import math
import jax
import jax.numpy as jnp
import numpy as np
from jax import lax

D = 8192
FF = 28672
RANK = 64
CAP = 8
REQUESTS = 32
VARIANTS = 16


def block_levels(own_key, shape, split, smallest, largest):
    loudness = 1.0
    for axis_at, blocks in split:
        steps = jax.random.uniform(jax.random.fold_in(jax.random.fold_in(own_key, 6), axis_at), (blocks,), jnp.float32, smallest / len(split), largest / len(split))
        loudness = loudness * jnp.repeat(jnp.exp(steps), shape[axis_at] // blocks).reshape((-1,) + (1,) * (len(shape) - 1 - axis_at))
    return loudness


def shared_out(key, own, number, rows, count, top, limit, lean):
    order = jax.random.permutation(key, count)
    heavy_load, usual = shares(count, rows * top, limit, lean, True), shares(count, rows * top, limit, lean, False)
    places = jnp.arange(count)

    def named(sizes, offset_by):
        used = int((sizes > 0).sum())
        fixed = max(1, used // 4)
        passed = fixed + (places - fixed + offset_by * (used - fixed)) % max(1, count - fixed)
        return jnp.zeros((count,), jnp.int32).at[order[jnp.where(places < fixed, places, passed)]].set(jnp.asarray(sizes, jnp.int32))

    sizes = jnp.where(number % 4 == 0, named(heavy_load, number // 4), named(usual, number - number // 4 - 1))
    mixed = jax.random.permutation(jax.random.fold_in(own, 3), count)
    donor, taker = mixed[0:count // 2 * 2:2], mixed[1:count // 2 * 2:2]
    margin = jnp.minimum(sizes[donor] - 1, limit - sizes[taker]) // 2
    margin = jnp.where((donor == order[0]) | (taker == order[0]) | (sizes[taker] == 0), 0, jnp.maximum(margin, 0))
    passed = jax.random.randint(jax.random.fold_in(own, 4), (count // 2,), 0, 1 << 20) % (margin + 1)
    sizes = sizes.at[donor].add(-passed).at[taker].add(passed)
    labels = jnp.searchsorted(jnp.cumsum(sizes), jnp.arange(rows * top), side="right").astype(jnp.int32)
    listing = labels.reshape(top, rows).T
    listing = listing[jax.random.permutation(jax.random.fold_in(own, 1), rows)]
    offset_by = jax.random.randint(jax.random.fold_in(own, 2), (rows, 1), 0, top)
    return jnp.take_along_axis(listing, (jnp.arange(top)[None, :] + offset_by) % top, axis=1)


def shares(amount, total, limit, lean, full):
    loads = [(1 << 20) // math.isqrt(standing ** lean) + 1 for standing in range(1, amount + 1)]
    largest = limit if full else min(limit, max(-(-total // amount), total * loads[0] // sum(loads)))
    least = 1 if total - largest >= amount - 1 else 0
    counts, rest = [largest] + [least] * (amount - 1), total - largest - least * (amount - 1)
    while rest > 0:
        movable = [i for i in range(1, amount) if counts[i] < largest] or [i for i in range(1, amount) if counts[i] < limit]
        mass, remaining = sum([loads[i] for i in movable]), rest
        for i in movable:
            extra = min(limit - counts[i], max(1, remaining * loads[i] // mass), rest)
            counts[i] = counts[i] + extra
            rest = rest - extra
    return np.array(counts)


def centred(key, extent, scale, bound, shards=(), held_as=jnp.bfloat16):
    result = scale * jax.random.normal(key, extent, jnp.float32)
    if shards:
        result = result * block_levels(key, extent, shards, -0.22, 0.18)
    return jnp.clip(result, -bound, bound).astype(held_as)


def setup_inputs(seed: int = 0, part: int = 0) -> dict:
    key_list = jax.random.split(jax.random.key(seed), 7)
    part_keys = jax.random.split(jax.random.fold_in(key_list[6], part), 7)
    hidden = centred(part_keys[0], (REQUESTS, FF), 1.0, 6.0, ((1, 16),))
    down_weight = centred(key_list[1], (FF, D), FF ** -0.5, 0.03125, ((0, 16),))
    shrink_factor = centred(key_list[2], (VARIANTS, RANK, FF), FF ** -0.5, 0.03125, ((0, 16),))
    expand_factor = centred(key_list[3], (VARIANTS, RANK, D), RANK ** -0.5, 0.75, ((0, 16),))
    variant_ids_keys = jax.random.split(jax.random.fold_in(part_keys[4], 1), REQUESTS // REQUESTS)
    variant_ids_turns = jax.random.permutation(jax.random.fold_in(part_keys[4], 3), REQUESTS // REQUESTS)
    variant_ids = jax.vmap(lambda own, number: shared_out(jax.random.fold_in(part_keys[4], 2), own, number, REQUESTS, VARIANTS, 1, CAP, 2))(variant_ids_keys, variant_ids_turns).reshape((REQUESTS, 1))
    owner = jax.random.permutation(key_list[5], VARIANTS).astype(jnp.int32)
    return dict(hidden=hidden, down_weight=down_weight, shrink_factor=shrink_factor, expand_factor=expand_factor, variant_ids=variant_ids, owner=owner)


def reference(hidden, down_weight, shrink_factor, expand_factor, variant_ids, owner):
    slot_of = owner[variant_ids[:, 0]].astype(jnp.int32)
    base = jnp.dot(hidden, down_weight, preferred_element_type=jnp.float32)

    def one_request(packed):
        act_row, slot_index = packed
        shrunk = jnp.dot(shrink_factor[slot_index], act_row, preferred_element_type=jnp.float32).astype(jnp.bfloat16)
        return jnp.dot(shrunk, expand_factor[slot_index], preferred_element_type=jnp.float32).astype(jnp.bfloat16)

    delta = lax.map(one_request, (hidden, slot_of))
    return (base + delta.astype(jnp.float32)).astype(jnp.bfloat16)
```

```python
import functools

import jax
import jax.numpy as jnp
from jax import lax
from jax.experimental import pallas as pl
from jax.experimental.pallas import tpu as pltpu
from jax.sharding import PartitionSpec as P

CAP = 8
F32 = jnp.float32
BF16 = jnp.bfloat16
MESH = pl.DeviceIdType.MESH


def iota(shape, axis):
    return lax.broadcasted_iota(jnp.int32, shape, axis)


def log2(n):
    return n.bit_length() - 1


def contract(a, b, da, db):
    return lax.dot_general(a, b, (((da,), (db,)), ((), ())), preferred_element_type=F32)


def kernel(n, chunks, vid, own, hid, w_hbm, s_hbm, e_hbm, out, wbuf, sbuf, ebuf, hperm, snd, rcv,
           part, arcv, bsnd, brcv, keep, csnd, crcv, wsem, ssem, esem, dss, drs, asem, arem, bsem,
           brem, csem, crem):
    me = lax.axis_index("tp")
    core, x, z = lax.rem(me, 2), lax.rem(me // 2, 2), me // 4
    nz = n // 4
    rows, cols = hid.shape
    per = rows // n
    group = nz * per
    half = cols // 2
    wide = wbuf.shape[2]
    folds = 16 // per
    narrow = wide // folds

    def load_w(c):
        at = pl.ds(pl.multiple_of(c * wide, wide), wide)
        return pltpu.make_async_copy(w_hbm.at[:, at], wbuf.at[c], wsem.at[c])

    load_s = pltpu.make_async_copy(s_hbm.at[0], sbuf, ssem)
    load_e = pltpu.make_async_copy(e_hbm.at[0], ebuf, esem)
    for c in range(chunks):
        load_w(c).start()
    load_s.start()
    load_e.start()

    barrier = pltpu.get_barrier_semaphore()

    @pl.loop(1, n)
    def _(d):
        pl.semaphore_signal(barrier, inc=1, device_id={"tp": lax.rem(me + d, n)}, device_id_type=MESH)

    variants = own.shape[1]
    named = vid[...] == iota((rows, variants), 1)
    holder = jnp.sum(jnp.where(named, own[...].astype(F32), 0.0), axis=1, keepdims=True)
    named = named.astype(F32).astype(BF16)
    same = contract(named, named, 1, 1)
    earlier = iota((rows, rows), 1) < iota((rows, rows), 0)
    order = jnp.sum(jnp.where(earlier, same, 0.0), axis=1, keepdims=True)
    slot = holder * CAP + order
    place = (slot == iota((rows, n * CAP), 1).astype(F32)).astype(F32).astype(BF16)
    halves = [
        contract(place, hid[:, h * half:(h + 1) * half], 0, 0).reshape(n, CAP, half) for h in range(2)
    ]
    snd[...] = jnp.concatenate(halves, axis=1).astype(BF16)
    rcv[0] = snd[me]

    at = iota((rows, rows), 0)
    r = at & (per - 1)
    z_of = lax.shift_right_logical(at, log2(per)) & (nz - 1)
    x_of = lax.shift_right_logical(at, log2(group)) & 1
    core_of = lax.shift_right_logical(at, log2(group) + 1)
    reorder = (((z_of * 2 + x_of) * 2 + core_of) * per + r == iota((rows, rows), 1))
    reorder = reorder.astype(F32).astype(BF16)
    hperm[...] = contract(reorder, hid[...], 1, 0).astype(BF16)
    mine = (slot == (iota((rows, CAP), 1) + me * CAP).astype(F32)).astype(F32).astype(BF16)
    spread = contract(reorder, mine, 1, 0).astype(BF16)

    pl.semaphore_wait(barrier, n - 1)

    def dispatch(d):
        to = lax.rem(me + d, n)
        return pltpu.make_async_remote_copy(
            src_ref=snd.at[to], dst_ref=rcv.at[d], send_sem=dss.at[d], recv_sem=drs.at[d],
            device_id={"tp": to}, device_id_type=MESH)

    @pl.loop(1, n)
    def _(d):
        dispatch(d).start()

    @pl.loop(0, chunks)
    def _(c):
        load_w(c).wait()
        total = jnp.dot(hperm[...], wbuf[c], preferred_element_type=F32)
        part[c] = total.reshape(2, 2, group, wide)

    load_s.wait()

    def shrink(d, total):
        start = lax.rem(me - d + n, n) * cols
        got = rcv[d]
        first = sbuf[:, pl.ds(pl.multiple_of(start, half), half)]
        second = sbuf[:, pl.ds(pl.multiple_of(start + half, half), half)]
        return total + contract(got, first, 1, 1)[:CAP] + contract(got, second, 1, 1)[CAP:]

    def arrived(d, total):
        dispatch(d).wait_recv()
        return shrink(d, total)

    shrunk = shrink(0, jnp.zeros((CAP, sbuf.shape[0]), F32))
    shrunk = lax.fori_loop(1, n, arrived, shrunk).astype(BF16)
    shrunk = contract(spread, shrunk, 1, 0).astype(BF16)
    load_e.wait()

    def to_core(c):
        return pltpu.make_async_remote_copy(
            src_ref=part.at[c, 1 - core], dst_ref=arcv.at[c], send_sem=asem.at[c],
            recv_sem=arem.at[c], device_id={"tp": me + 1 - 2 * core}, device_id_type=MESH)

    def to_x(c):
        return pltpu.make_async_remote_copy(
            src_ref=bsnd.at[c], dst_ref=brcv.at[c], send_sem=bsem.at[c], recv_sem=brem.at[c],
            device_id={"tp": me + 2 - 4 * x}, device_id_type=MESH)

    def to_z(c, d):
        to = lax.rem(z + d, nz)
        return pltpu.make_async_remote_copy(
            src_ref=csnd.at[c, to], dst_ref=crcv.at[c, d - 1], send_sem=csem.at[c, d - 1],
            recv_sem=crem.at[c, d - 1], device_id={"tp": me + (to - z) * 4}, device_id_type=MESH)

    @pl.loop(0, chunks)
    def _(c):
        at = pl.ds(pl.multiple_of(c * wide, wide), wide)
        delta = jnp.dot(shrunk, ebuf[:, at], preferred_element_type=F32).astype(BF16).astype(F32)
        part[c] = part[c] + delta.reshape(2, 2, group, wide)
        to_core(c).start()

    @pl.loop(0, chunks)
    def _(c):
        to_core(c).wait_recv()
        away = part[c, core, 1 - x] + arcv[c, 1 - x]
        away = jnp.concatenate([away[:, :wide // 2], away[:, wide // 2:]], axis=0)
        bsnd[c] = away.astype(BF16)
        to_x(c).start()
        keep[c] = part[c, core, x] + arcv[c, x]

    size = folds * group
    at = iota((size, size), 0)
    r = at & (per - 1)
    fold = lax.shift_right_logical(at, log2(per)) & (folds - 1)
    z_of = lax.shift_right_logical(at, log2(per * folds))
    refold = ((fold * nz + z_of) * per + r == iota((size, size), 1)).astype(F32).astype(BF16)

    @pl.loop(0, chunks)
    def _(c):
        to_x(c).wait_recv()
        got = brcv[c].astype(F32)
        total = keep[c] + jnp.concatenate([got[:group], got[group:]], axis=1)
        folded = jnp.concatenate(
            [total[:, j * narrow:(j + 1) * narrow] for j in range(folds)], axis=0).astype(BF16)
        csnd[c] = contract(refold, folded, 1, 0).astype(BF16).reshape(nz, 16, narrow)
        for d in range(1, nz):
            to_z(c, d).start()

    @pl.loop(0, chunks)
    def _(c):
        total = csnd[c, z].astype(F32)
        for d in range(1, nz):
            to_z(c, d).wait_recv()
            total = total + crcv[c, d - 1].astype(F32)
        row = jnp.concatenate([total[j * per:(j + 1) * per] for j in range(folds)], axis=1)
        out[:, pl.ds(pl.multiple_of(c * wide, wide), wide)] = row.astype(BF16)

    @pl.loop(1, n)
    def _(d):
        dispatch(d).wait_send()

    @pl.loop(0, chunks)
    def _(c):
        to_core(c).wait_send()
        to_x(c).wait_send()
        for d in range(1, nz):
            to_z(c, d).wait_send()


def fits(n, rows, cols, width):
    per = rows // n
    return (n % 4 == 0 and cols % 256 == 0 and width % 1024 == 0 and per in (1, 2, 4, 8, 16)
            and rows == n * per and (n // 4) * per == 8)


def fused(hidden, down_weight, shrink_factor, expand_factor, variant_ids, owner):
    n = lax.axis_size("tp")
    rows, cols = hidden.shape
    rank, depth = shrink_factor.shape[1:]
    width = down_weight.shape[1]
    wide = 1024
    chunks = width // wide
    nz = n // 4
    per = rows // n
    group = nz * per
    narrow = wide * per // 16
    vmem = pl.BlockSpec(memory_space=pltpu.VMEM)
    hbm = pl.BlockSpec(memory_space=pl.ANY)
    dma = pltpu.SemaphoreType.DMA
    return pl.pallas_call(
        functools.partial(kernel, n, chunks),
        out_shape=jax.ShapeDtypeStruct((per, width), BF16),
        in_specs=[vmem, vmem, vmem, hbm, hbm, hbm],
        out_specs=vmem,
        scratch_shapes=[
            pltpu.VMEM((chunks, cols, wide), BF16),
            pltpu.VMEM((rank, depth), BF16),
            pltpu.VMEM((rank, width), BF16),
            pltpu.VMEM((rows, cols), BF16),
            pltpu.VMEM((n, 2 * CAP, cols // 2), BF16),
            pltpu.VMEM((n, 2 * CAP, cols // 2), BF16),
            pltpu.VMEM((chunks, 2, 2, group, wide), F32),
            pltpu.VMEM((chunks, 2, group, wide), F32),
            pltpu.VMEM((chunks, 2 * group, wide // 2), BF16),
            pltpu.VMEM((chunks, 2 * group, wide // 2), BF16),
            pltpu.VMEM((chunks, group, wide), F32),
            pltpu.VMEM((chunks, nz, 16, narrow), BF16),
            pltpu.VMEM((chunks, nz - 1, 16, narrow), BF16),
            dma((chunks,)), dma(()), dma(()), dma((n,)), dma((n,)),
            dma((chunks,)), dma((chunks,)), dma((chunks,)), dma((chunks,)),
            dma((chunks, nz - 1)), dma((chunks, nz - 1)),
        ],
        compiler_params=pltpu.CompilerParams(
            collective_id=0, has_side_effects=True, vmem_limit_bytes=56 * 2**20),
        name="fused",
    )(variant_ids, owner.reshape(1, -1), hidden, down_weight, shrink_factor, expand_factor)


def general(hidden, down_weight, shrink_factor, expand_factor, variant_ids, owner):
    group_size = lax.axis_size("tp")
    my_index = lax.axis_index("tp")
    row_count = hidden.shape[0]
    col_count = hidden.shape[1]
    width_out = expand_factor.shape[2]
    rank_width = shrink_factor.shape[1]
    capacity = CAP
    variant_of = variant_ids[:, 0]
    holder = owner[variant_of]
    held_here = holder == my_index
    onehot = (variant_of[:, None] == jnp.arange(owner.shape[0], dtype=jnp.int32)[None, :]).astype(
        jnp.int32
    )
    earlier = jnp.cumsum(onehot, axis=0) - onehot
    order_in = jnp.sum(earlier * onehot, axis=1)
    request_index = jnp.arange(row_count, dtype=jnp.int32)
    slices = lax.all_to_all(shrink_factor, "tp", split_axis=2, concat_axis=0, tiled=True)
    all_rows = slices.reshape(group_size * rank_width, col_count)
    every_slot = lax.dot_general(
        hidden, all_rows, (((1,), (1,)), ((), ())), preferred_element_type=jnp.float32
    )
    every_slot = every_slot.reshape(row_count, group_size, rank_width)
    chosen = holder[:, None] == jnp.arange(group_size, dtype=jnp.int32)[None, :]
    partial_value = jnp.sum(jnp.where(chosen[:, :, None], every_slot, jnp.float32(0.0)), axis=1)
    shrunk = lax.psum(partial_value, "tp").astype(jnp.bfloat16)
    source = jnp.full((capacity,), row_count, jnp.int32)
    source = source.at[jnp.where(held_here, order_in, capacity)].set(request_index, mode="drop")
    padded_shrunk = jnp.concatenate([shrunk, jnp.zeros((1, shrunk.shape[1]), jnp.bfloat16)], axis=0)
    delta_rows = jnp.dot(
        padded_shrunk[source], expand_factor[0], preferred_element_type=jnp.float32
    ).astype(jnp.bfloat16)
    delta_table = jnp.concatenate([delta_rows, jnp.zeros((1, width_out), jnp.bfloat16)], axis=0)
    pick_index = jnp.where(held_here, order_in, capacity)
    block_base = jnp.dot(hidden, down_weight, preferred_element_type=jnp.float32)
    summed = lax.psum_scatter(
        block_base + delta_table[pick_index].astype(jnp.float32),
        "tp",
        scatter_dimension=0,
        tiled=True,
    )
    return summed.astype(jnp.bfloat16)


def local(hidden, down_weight, shrink_factor, expand_factor, variant_ids, owner):
    n = lax.axis_size("tp")
    form = fused if fits(n, *hidden.shape, down_weight.shape[1]) else general
    return form(hidden, down_weight, shrink_factor, expand_factor, variant_ids, owner)


def solution(mesh):
    in_specs = (
        P("rep", "tp"),
        P("tp", None),
        P("tp", None, None),
        P("tp", None, None),
        P("rep", None),
        P(),
    )
    out_specs = P(("rep", "tp"), None)
    return jax.shard_map(local, mesh=mesh, in_specs=in_specs, out_specs=out_specs, check_vma=False)
```

```python
import functools

import jax
import jax.numpy as jnp
from jax import lax
from jax.experimental import pallas as pl
from jax.experimental.pallas import tpu as pltpu
from jax.sharding import PartitionSpec as P

CAP = 8
F32 = jnp.float32
BF16 = jnp.bfloat16
MESH = pl.DeviceIdType.MESH


def iota(shape, axis):
    return lax.broadcasted_iota(jnp.int32, shape, axis)


def log2(n):
    return n.bit_length() - 1


def contract(a, b, da, db):
    return lax.dot_general(a, b, (((da,), (db,)), ((), ())), preferred_element_type=F32)


def kernel(n, chunks, vid, own, hid, w_hbm, s_hbm, e_hbm, out, wbuf, sbuf, ebuf, hperm, snd, rcv,
           part, arcv, bsnd, brcv, keep, csnd, crcv, wsem, ssem, esem, dss, drs, asem, arem, bsem,
           brem, csem, crem):
    me = lax.axis_index("tp")
    core, x, z = lax.rem(me, 2), lax.rem(me // 2, 2), me // 4
    nz = n // 4
    rows, cols = hid.shape
    per = rows // n
    group = nz * per
    half = cols // 2
    wide = wbuf.shape[2]
    folds = 16 // per
    narrow = wide // folds

    def load_w(c):
        at = pl.ds(pl.multiple_of(c * wide, wide), wide)
        return pltpu.make_async_copy(w_hbm.at[:, at], wbuf.at[c], wsem.at[c])

    load_s = pltpu.make_async_copy(s_hbm.at[0], sbuf, ssem)
    load_e = pltpu.make_async_copy(e_hbm.at[0], ebuf, esem)
    for c in range(chunks):
        load_w(c).start()
    load_s.start()
    load_e.start()

    barrier = pltpu.get_barrier_semaphore()

    @pl.loop(1, n)
    def _(d):
        pl.semaphore_signal(barrier, inc=1, device_id={"tp": lax.rem(me + d, n)}, device_id_type=MESH)

    variants = own.shape[1]
    named = vid[...] == iota((variants, rows), 0)
    named = named.astype(F32).astype(BF16)
    holder = contract(own[...].astype(F32).astype(BF16), named, 1, 0)
    same = contract(named, named, 0, 0)
    earlier = iota((rows, rows), 0) < iota((rows, rows), 1)
    order = jnp.sum(jnp.where(earlier, same, 0.0), axis=0, keepdims=True)
    slot = holder * CAP + order
    place = (slot == iota((n * CAP, rows), 0).astype(F32)).astype(F32).astype(BF16)
    halves = [
        contract(place, hid[:, h * half:(h + 1) * half], 1, 0).reshape(n, CAP, half) for h in range(2)
    ]
    snd[...] = jnp.concatenate(halves, axis=1).astype(BF16)
    rcv[0] = snd[me]

    at = iota((rows, rows), 0)
    r = at & (per - 1)
    z_of = lax.shift_right_logical(at, log2(per)) & (nz - 1)
    x_of = lax.shift_right_logical(at, log2(group)) & 1
    core_of = lax.shift_right_logical(at, log2(group) + 1)
    reorder = (((z_of * 2 + x_of) * 2 + core_of) * per + r == iota((rows, rows), 1))
    reorder = reorder.astype(F32).astype(BF16)
    hperm[...] = contract(reorder, hid[...], 1, 0).astype(BF16)
    mine = (slot == (iota((CAP, rows), 0) + me * CAP).astype(F32)).astype(F32).astype(BF16)
    spread = contract(reorder, mine, 1, 1).astype(BF16)

    pl.semaphore_wait(barrier, n - 1)

    def dispatch(d):
        to = lax.rem(me + d, n)
        return pltpu.make_async_remote_copy(
            src_ref=snd.at[to], dst_ref=rcv.at[d], send_sem=dss.at[d], recv_sem=drs.at[d],
            device_id={"tp": to}, device_id_type=MESH)

    order_out = ((n // 2, n), (n // 4, n // 2), (1, n // 4))
    for first, last in order_out:
        @pl.loop(first, last)
        def _(d):
            dispatch(d).start()

    @pl.loop(0, chunks)
    def _(c):
        load_w(c).wait()
        total = jnp.dot(hperm[...], wbuf[c], preferred_element_type=F32)
        part[c] = total.reshape(2, 2, group, wide)

    load_s.wait()

    def shrink(d, total):
        start = lax.rem(me - d + n, n) * cols
        got = rcv[d]
        first = sbuf[:, pl.ds(pl.multiple_of(start, half), half)]
        second = sbuf[:, pl.ds(pl.multiple_of(start + half, half), half)]
        return total + contract(got, first, 1, 1)[:CAP] + contract(got, second, 1, 1)[CAP:]

    def arrived(d, total):
        dispatch(d).wait_recv()
        return shrink(d, total)

    shrunk = shrink(0, jnp.zeros((CAP, sbuf.shape[0]), F32))
    for first, last in order_out:
        shrunk = lax.fori_loop(first, last, arrived, shrunk)
    shrunk = contract(spread, shrunk.astype(BF16), 1, 0).astype(BF16)
    load_e.wait()

    def to_core(c):
        return pltpu.make_async_remote_copy(
            src_ref=part.at[c, 1 - core], dst_ref=arcv.at[c], send_sem=asem.at[c],
            recv_sem=arem.at[c], device_id={"tp": me + 1 - 2 * core}, device_id_type=MESH)

    def to_x(c):
        return pltpu.make_async_remote_copy(
            src_ref=bsnd.at[c], dst_ref=brcv.at[c], send_sem=bsem.at[c], recv_sem=brem.at[c],
            device_id={"tp": me + 2 - 4 * x}, device_id_type=MESH)

    def to_z(c, d):
        to = lax.rem(z + d, nz)
        return pltpu.make_async_remote_copy(
            src_ref=csnd.at[c, to], dst_ref=crcv.at[c, d - 1], send_sem=csem.at[c, d - 1],
            recv_sem=crem.at[c, d - 1], device_id={"tp": me + (to - z) * 4}, device_id_type=MESH)

    @pl.loop(0, chunks)
    def _(c):
        at = pl.ds(pl.multiple_of(c * wide, wide), wide)
        delta = jnp.dot(shrunk, ebuf[:, at], preferred_element_type=F32).astype(BF16).astype(F32)
        part[c] = part[c] + delta.reshape(2, 2, group, wide)
        to_core(c).start()

    @pl.loop(0, chunks)
    def _(c):
        to_core(c).wait_recv()
        away = part[c, core, 1 - x] + arcv[c, 1 - x]
        away = jnp.concatenate([away[:, :wide // 2], away[:, wide // 2:]], axis=0)
        bsnd[c] = away.astype(BF16)
        to_x(c).start()
        keep[c] = part[c, core, x] + arcv[c, x]

    size = folds * group
    at = iota((size, size), 0)
    r = at & (per - 1)
    fold = lax.shift_right_logical(at, log2(per)) & (folds - 1)
    z_of = lax.shift_right_logical(at, log2(per * folds))
    refold = ((fold * nz + z_of) * per + r == iota((size, size), 1)).astype(F32).astype(BF16)

    @pl.loop(0, chunks)
    def _(c):
        to_x(c).wait_recv()
        got = brcv[c].astype(F32)
        total = keep[c] + jnp.concatenate([got[:group], got[group:]], axis=1)
        folded = jnp.concatenate(
            [total[:, j * narrow:(j + 1) * narrow] for j in range(folds)], axis=0).astype(BF16)
        csnd[c] = contract(refold, folded, 1, 0).astype(BF16).reshape(nz, 16, narrow)
        for d in range(1, nz):
            to_z(c, d).start()

    @pl.loop(0, chunks)
    def _(c):
        total = csnd[c, z].astype(F32)
        for d in range(1, nz):
            to_z(c, d).wait_recv()
            total = total + crcv[c, d - 1].astype(F32)
        row = jnp.concatenate([total[j * per:(j + 1) * per] for j in range(folds)], axis=1)
        out[:, pl.ds(pl.multiple_of(c * wide, wide), wide)] = row.astype(BF16)

    @pl.loop(1, n)
    def _(d):
        dispatch(d).wait_send()

    @pl.loop(0, chunks)
    def _(c):
        to_core(c).wait_send()
        to_x(c).wait_send()
        for d in range(1, nz):
            to_z(c, d).wait_send()


def fits(n, rows, cols, width):
    per = rows // n
    return (n % 4 == 0 and n <= 256 and cols % 256 == 0 and width % 2048 == 0 and per in (1, 2, 4, 8, 16)
            and rows == n * per and (n // 4) * per == 8)


def fused(hidden, down_weight, shrink_factor, expand_factor, variant_ids, owner):
    n = lax.axis_size("tp")
    rows, cols = hidden.shape
    rank, depth = shrink_factor.shape[1:]
    width = down_weight.shape[1]
    wide = 2048
    chunks = width // wide
    nz = n // 4
    per = rows // n
    group = nz * per
    narrow = wide * per // 16
    vmem = pl.BlockSpec(memory_space=pltpu.VMEM)
    hbm = pl.BlockSpec(memory_space=pl.ANY)
    dma = pltpu.SemaphoreType.DMA
    return pl.pallas_call(
        functools.partial(kernel, n, chunks),
        out_shape=jax.ShapeDtypeStruct((per, width), BF16),
        in_specs=[vmem, vmem, vmem, hbm, hbm, hbm],
        out_specs=vmem,
        scratch_shapes=[
            pltpu.VMEM((chunks, cols, wide), BF16),
            pltpu.VMEM((rank, depth), BF16),
            pltpu.VMEM((rank, width), BF16),
            pltpu.VMEM((rows, cols), BF16),
            pltpu.VMEM((n, 2 * CAP, cols // 2), BF16),
            pltpu.VMEM((n, 2 * CAP, cols // 2), BF16),
            pltpu.VMEM((chunks, 2, 2, group, wide), F32),
            pltpu.VMEM((chunks, 2, group, wide), F32),
            pltpu.VMEM((chunks, 2 * group, wide // 2), BF16),
            pltpu.VMEM((chunks, 2 * group, wide // 2), BF16),
            pltpu.VMEM((chunks, group, wide), F32),
            pltpu.VMEM((chunks, nz, 16, narrow), BF16),
            pltpu.VMEM((chunks, nz - 1, 16, narrow), BF16),
            dma((chunks,)), dma(()), dma(()), dma((n,)), dma((n,)),
            dma((chunks,)), dma((chunks,)), dma((chunks,)), dma((chunks,)),
            dma((chunks, nz - 1)), dma((chunks, nz - 1)),
        ],
        compiler_params=pltpu.CompilerParams(
            collective_id=0, has_side_effects=True, vmem_limit_bytes=56 * 2**20),
        name="fused",
    )(variant_ids.reshape(1, -1), owner.reshape(1, -1), hidden, down_weight, shrink_factor, expand_factor)


def general(hidden, down_weight, shrink_factor, expand_factor, variant_ids, owner):
    group_size = lax.axis_size("tp")
    my_index = lax.axis_index("tp")
    row_count = hidden.shape[0]
    col_count = hidden.shape[1]
    width_out = expand_factor.shape[2]
    rank_width = shrink_factor.shape[1]
    capacity = CAP
    variant_of = variant_ids[:, 0]
    holder = owner[variant_of]
    held_here = holder == my_index
    onehot = (variant_of[:, None] == jnp.arange(owner.shape[0], dtype=jnp.int32)[None, :]).astype(
        jnp.int32
    )
    earlier = jnp.cumsum(onehot, axis=0) - onehot
    order_in = jnp.sum(earlier * onehot, axis=1)
    request_index = jnp.arange(row_count, dtype=jnp.int32)
    slices = lax.all_to_all(shrink_factor, "tp", split_axis=2, concat_axis=0, tiled=True)
    all_rows = slices.reshape(group_size * rank_width, col_count)
    every_slot = lax.dot_general(
        hidden, all_rows, (((1,), (1,)), ((), ())), preferred_element_type=jnp.float32
    )
    every_slot = every_slot.reshape(row_count, group_size, rank_width)
    chosen = holder[:, None] == jnp.arange(group_size, dtype=jnp.int32)[None, :]
    partial_value = jnp.sum(jnp.where(chosen[:, :, None], every_slot, jnp.float32(0.0)), axis=1)
    shrunk = lax.psum(partial_value, "tp").astype(jnp.bfloat16)
    source = jnp.full((capacity,), row_count, jnp.int32)
    source = source.at[jnp.where(held_here, order_in, capacity)].set(request_index, mode="drop")
    padded_shrunk = jnp.concatenate([shrunk, jnp.zeros((1, shrunk.shape[1]), jnp.bfloat16)], axis=0)
    delta_rows = jnp.dot(
        padded_shrunk[source], expand_factor[0], preferred_element_type=jnp.float32
    ).astype(jnp.bfloat16)
    delta_table = jnp.concatenate([delta_rows, jnp.zeros((1, width_out), jnp.bfloat16)], axis=0)
    pick_index = jnp.where(held_here, order_in, capacity)
    block_base = jnp.dot(hidden, down_weight, preferred_element_type=jnp.float32)
    summed = lax.psum_scatter(
        block_base + delta_table[pick_index].astype(jnp.float32),
        "tp",
        scatter_dimension=0,
        tiled=True,
    )
    return summed.astype(jnp.bfloat16)


def local(hidden, down_weight, shrink_factor, expand_factor, variant_ids, owner):
    n = lax.axis_size("tp")
    form = fused if fits(n, *hidden.shape, down_weight.shape[1]) else general
    return form(hidden, down_weight, shrink_factor, expand_factor, variant_ids, owner)


def solution(mesh):
    in_specs = (
        P("rep", "tp"),
        P("tp", None),
        P("tp", None, None),
        P("tp", None, None),
        P("rep", None),
        P(),
    )
    out_specs = P(("rep", "tp"), None)
    return jax.shard_map(local, mesh=mesh, in_specs=in_specs, out_specs=out_specs, check_vma=False)
```

```python
import functools

import jax
import jax.numpy as jnp
from jax import lax
from jax.experimental import pallas as pl
from jax.experimental.pallas import tpu as pltpu
from jax.sharding import PartitionSpec as P

CAP = 8
F32 = jnp.float32
BF16 = jnp.bfloat16
MESH = pl.DeviceIdType.MESH


def iota(shape, axis):
    return lax.broadcasted_iota(jnp.int32, shape, axis)


def log2(n):
    return n.bit_length() - 1


def contract(a, b, da, db):
    return lax.dot_general(a, b, (((da,), (db,)), ((), ())), preferred_element_type=F32)


def kernel(n, chunks, vid, own, hid, w_hbm, s_hbm, e_hbm, out, wbuf, sbuf, ebuf, hperm, snd, rcv,
           part, arcv, bsnd, brcv, keep, csnd, crcv, wsem, ssem, esem, dss, drs, asem, arem, bsem,
           brem, csem, crem):
    me = lax.axis_index("tp")
    core, x, z = lax.rem(me, 2), lax.rem(me // 2, 2), me // 4
    nz = n // 4
    rows, cols = hid.shape
    per = rows // n
    group = nz * per
    half = cols // 2
    wide = wbuf.shape[2]
    folds = 16 // per
    narrow = wide // folds

    def load_w(c):
        at = pl.ds(pl.multiple_of(c * wide, wide), wide)
        return pltpu.make_async_copy(w_hbm.at[:, at], wbuf.at[c], wsem.at[c])

    load_s = pltpu.make_async_copy(s_hbm.at[0], sbuf, ssem)
    load_e = pltpu.make_async_copy(e_hbm.at[0], ebuf, esem)
    for c in range(chunks):
        load_w(c).start()
    load_s.start()
    load_e.start()

    barrier = pltpu.get_barrier_semaphore()

    @pl.loop(1, n)
    def _(d):
        pl.semaphore_signal(barrier, inc=1, device_id={"tp": lax.rem(me + d, n)}, device_id_type=MESH)

    variants = own.shape[1]
    named = vid[...] == iota((variants, rows), 0)
    named = named.astype(F32).astype(BF16)
    holder = contract(own[...].astype(F32).astype(BF16), named, 1, 0)
    same = contract(named, named, 0, 0)
    earlier = iota((rows, rows), 0) < iota((rows, rows), 1)
    order = jnp.sum(jnp.where(earlier, same, 0.0), axis=0, keepdims=True)
    slot = holder * CAP + order
    place = (slot == iota((n * CAP, rows), 0).astype(F32)).astype(F32).astype(BF16)
    halves = [
        contract(place, hid[:, h * half:(h + 1) * half], 1, 0).reshape(n, CAP, half) for h in range(2)
    ]
    snd[...] = jnp.concatenate(halves, axis=1).astype(BF16)
    rcv[0] = snd[me]

    at = iota((rows, rows), 0)
    r = at & (per - 1)
    z_of = lax.shift_right_logical(at, log2(per)) & (nz - 1)
    x_of = lax.shift_right_logical(at, log2(group)) & 1
    core_of = lax.shift_right_logical(at, log2(group) + 1)
    reorder = (((z_of * 2 + x_of) * 2 + core_of) * per + r == iota((rows, rows), 1))
    reorder = reorder.astype(F32).astype(BF16)
    hperm[...] = contract(reorder, hid[...], 1, 0).astype(BF16)
    mine = (slot == (iota((CAP, rows), 0) + me * CAP).astype(F32)).astype(F32).astype(BF16)
    spread = contract(reorder, mine, 1, 1).astype(BF16)

    pl.semaphore_wait(barrier, n - 1)

    def dispatch(d):
        to = lax.rem(me + d, n)
        return pltpu.make_async_remote_copy(
            src_ref=snd.at[to], dst_ref=rcv.at[d], send_sem=dss.at[d], recv_sem=drs.at[d],
            device_id={"tp": to}, device_id_type=MESH)

    order_out = ((1, n // 4), (n // 2, n), (n // 4, n // 2))
    for first, last in order_out:
        @pl.loop(first, last)
        def _(d):
            dispatch(d).start()

    @pl.loop(0, chunks)
    def _(c):
        load_w(c).wait()
        total = jnp.dot(hperm[...], wbuf[c], preferred_element_type=F32)
        part[c] = total.reshape(2, 2, group, wide)

    load_s.wait()

    def shrink(d, totals):
        start = lax.rem(me - d + n, n) * cols
        got = rcv[d]
        first = sbuf[:, pl.ds(pl.multiple_of(start, half), half)]
        second = sbuf[:, pl.ds(pl.multiple_of(start + half, half), half)]
        return totals[0] + contract(got, first, 1, 1), totals[1] + contract(got, second, 1, 1)

    zero = jnp.zeros((2 * CAP, sbuf.shape[0]), F32)
    totals = shrink(0, (zero, zero))
    for first, last in order_out:
        @pl.loop(first, last)
        def _(d):
            dispatch(d).wait_recv()

        for d in range(first, last):
            totals = shrink(d, totals)
    top, low = totals
    shrunk = (top[:CAP] + low[CAP:]).astype(BF16)
    shrunk = contract(spread, shrunk, 1, 0).astype(BF16)
    load_e.wait()

    def to_core(c):
        return pltpu.make_async_remote_copy(
            src_ref=part.at[c, 1 - core], dst_ref=arcv.at[c], send_sem=asem.at[c],
            recv_sem=arem.at[c], device_id={"tp": me + 1 - 2 * core}, device_id_type=MESH)

    def to_x(c):
        return pltpu.make_async_remote_copy(
            src_ref=bsnd.at[c], dst_ref=brcv.at[c], send_sem=bsem.at[c], recv_sem=brem.at[c],
            device_id={"tp": me + 2 - 4 * x}, device_id_type=MESH)

    def to_z(c, d):
        to = lax.rem(z + d, nz)
        return pltpu.make_async_remote_copy(
            src_ref=csnd.at[c, to], dst_ref=crcv.at[c, d - 1], send_sem=csem.at[c, d - 1],
            recv_sem=crem.at[c, d - 1], device_id={"tp": me + (to - z) * 4}, device_id_type=MESH)

    @pl.loop(0, chunks)
    def _(c):
        at = pl.ds(pl.multiple_of(c * wide, wide), wide)
        delta = jnp.dot(shrunk, ebuf[:, at], preferred_element_type=F32).astype(BF16).astype(F32)
        part[c] = part[c] + delta.reshape(2, 2, group, wide)
        to_core(c).start()

    @pl.loop(0, chunks)
    def _(c):
        to_core(c).wait_recv()
        away = part[c, core, 1 - x] + arcv[c, 1 - x]
        away = jnp.concatenate([away[:, :wide // 2], away[:, wide // 2:]], axis=0)
        bsnd[c] = away.astype(BF16)
        to_x(c).start()
        keep[c] = part[c, core, x] + arcv[c, x]

    size = folds * group
    at = iota((size, size), 0)
    r = at & (per - 1)
    fold = lax.shift_right_logical(at, log2(per)) & (folds - 1)
    z_of = lax.shift_right_logical(at, log2(per * folds))
    refold = ((fold * nz + z_of) * per + r == iota((size, size), 1)).astype(F32).astype(BF16)

    @pl.loop(0, chunks)
    def _(c):
        to_x(c).wait_recv()
        got = brcv[c].astype(F32)
        total = keep[c] + jnp.concatenate([got[:group], got[group:]], axis=1)
        folded = jnp.concatenate(
            [total[:, j * narrow:(j + 1) * narrow] for j in range(folds)], axis=0).astype(BF16)
        csnd[c] = contract(refold, folded, 1, 0).astype(BF16).reshape(nz, 16, narrow)
        for d in range(1, nz):
            to_z(c, d).start()

    @pl.loop(0, chunks)
    def _(c):
        total = csnd[c, z].astype(F32)
        for d in range(1, nz):
            to_z(c, d).wait_recv()
            total = total + crcv[c, d - 1].astype(F32)
        row = jnp.concatenate([total[j * per:(j + 1) * per] for j in range(folds)], axis=1)
        out[:, pl.ds(pl.multiple_of(c * wide, wide), wide)] = row.astype(BF16)

    @pl.loop(1, n)
    def _(d):
        dispatch(d).wait_send()

    @pl.loop(0, chunks)
    def _(c):
        to_core(c).wait_send()
        to_x(c).wait_send()
        for d in range(1, nz):
            to_z(c, d).wait_send()


def fits(n, rows, cols, width):
    per = rows // n
    return (n % 4 == 0 and n <= 256 and cols % 256 == 0 and width % 2048 == 0 and per in (1, 2, 4, 8, 16)
            and rows == n * per and (n // 4) * per == 8)


def fused(hidden, down_weight, shrink_factor, expand_factor, variant_ids, owner):
    n = lax.axis_size("tp")
    rows, cols = hidden.shape
    rank, depth = shrink_factor.shape[1:]
    width = down_weight.shape[1]
    wide = 2048
    chunks = width // wide
    nz = n // 4
    per = rows // n
    group = nz * per
    narrow = wide * per // 16
    vmem = pl.BlockSpec(memory_space=pltpu.VMEM)
    hbm = pl.BlockSpec(memory_space=pl.ANY)
    dma = pltpu.SemaphoreType.DMA
    return pl.pallas_call(
        functools.partial(kernel, n, chunks),
        out_shape=jax.ShapeDtypeStruct((per, width), BF16),
        in_specs=[vmem, vmem, vmem, hbm, hbm, hbm],
        out_specs=vmem,
        scratch_shapes=[
            pltpu.VMEM((chunks, cols, wide), BF16),
            pltpu.VMEM((rank, depth), BF16),
            pltpu.VMEM((rank, width), BF16),
            pltpu.VMEM((rows, cols), BF16),
            pltpu.VMEM((n, 2 * CAP, cols // 2), BF16),
            pltpu.VMEM((n, 2 * CAP, cols // 2), BF16),
            pltpu.VMEM((chunks, 2, 2, group, wide), F32),
            pltpu.VMEM((chunks, 2, group, wide), F32),
            pltpu.VMEM((chunks, 2 * group, wide // 2), BF16),
            pltpu.VMEM((chunks, 2 * group, wide // 2), BF16),
            pltpu.VMEM((chunks, group, wide), F32),
            pltpu.VMEM((chunks, nz, 16, narrow), BF16),
            pltpu.VMEM((chunks, nz - 1, 16, narrow), BF16),
            dma((chunks,)), dma(()), dma(()), dma((n,)), dma((n,)),
            dma((chunks,)), dma((chunks,)), dma((chunks,)), dma((chunks,)),
            dma((chunks, nz - 1)), dma((chunks, nz - 1)),
        ],
        compiler_params=pltpu.CompilerParams(
            collective_id=0, has_side_effects=True, vmem_limit_bytes=56 * 2**20),
        name="fused",
    )(variant_ids.reshape(1, -1), owner.reshape(1, -1), hidden, down_weight, shrink_factor, expand_factor)


def general(hidden, down_weight, shrink_factor, expand_factor, variant_ids, owner):
    group_size = lax.axis_size("tp")
    my_index = lax.axis_index("tp")
    row_count = hidden.shape[0]
    col_count = hidden.shape[1]
    width_out = expand_factor.shape[2]
    rank_width = shrink_factor.shape[1]
    capacity = CAP
    variant_of = variant_ids[:, 0]
    holder = owner[variant_of]
    held_here = holder == my_index
    onehot = (variant_of[:, None] == jnp.arange(owner.shape[0], dtype=jnp.int32)[None, :]).astype(
        jnp.int32
    )
    earlier = jnp.cumsum(onehot, axis=0) - onehot
    order_in = jnp.sum(earlier * onehot, axis=1)
    request_index = jnp.arange(row_count, dtype=jnp.int32)
    slices = lax.all_to_all(shrink_factor, "tp", split_axis=2, concat_axis=0, tiled=True)
    all_rows = slices.reshape(group_size * rank_width, col_count)
    every_slot = lax.dot_general(
        hidden, all_rows, (((1,), (1,)), ((), ())), preferred_element_type=jnp.float32
    )
    every_slot = every_slot.reshape(row_count, group_size, rank_width)
    chosen = holder[:, None] == jnp.arange(group_size, dtype=jnp.int32)[None, :]
    partial_value = jnp.sum(jnp.where(chosen[:, :, None], every_slot, jnp.float32(0.0)), axis=1)
    shrunk = lax.psum(partial_value, "tp").astype(jnp.bfloat16)
    source = jnp.full((capacity,), row_count, jnp.int32)
    source = source.at[jnp.where(held_here, order_in, capacity)].set(request_index, mode="drop")
    padded_shrunk = jnp.concatenate([shrunk, jnp.zeros((1, shrunk.shape[1]), jnp.bfloat16)], axis=0)
    delta_rows = jnp.dot(
        padded_shrunk[source], expand_factor[0], preferred_element_type=jnp.float32
    ).astype(jnp.bfloat16)
    delta_table = jnp.concatenate([delta_rows, jnp.zeros((1, width_out), jnp.bfloat16)], axis=0)
    pick_index = jnp.where(held_here, order_in, capacity)
    block_base = jnp.dot(hidden, down_weight, preferred_element_type=jnp.float32)
    summed = lax.psum_scatter(
        block_base + delta_table[pick_index].astype(jnp.float32),
        "tp",
        scatter_dimension=0,
        tiled=True,
    )
    return summed.astype(jnp.bfloat16)


def local(hidden, down_weight, shrink_factor, expand_factor, variant_ids, owner):
    n = lax.axis_size("tp")
    form = fused if fits(n, *hidden.shape, down_weight.shape[1]) else general
    return form(hidden, down_weight, shrink_factor, expand_factor, variant_ids, owner)


def solution(mesh):
    in_specs = (
        P("rep", "tp"),
        P("tp", None),
        P("tp", None, None),
        P("tp", None, None),
        P("rep", None),
        P(),
    )
    out_specs = P(("rep", "tp"), None)
    return jax.shard_map(local, mesh=mesh, in_specs=in_specs, out_specs=out_specs, check_vma=False)
```

```python
import functools

import jax
import jax.numpy as jnp
from jax import lax
from jax.experimental import pallas as pl
from jax.experimental.pallas import tpu as pltpu
from jax.sharding import PartitionSpec as P

CAP = 8
F32 = jnp.float32
BF16 = jnp.bfloat16
MESH = pl.DeviceIdType.MESH


def iota(shape, axis):
    return lax.broadcasted_iota(jnp.int32, shape, axis)


def log2(n):
    return n.bit_length() - 1


def contract(a, b, da, db):
    return lax.dot_general(a, b, (((da,), (db,)), ((), ())), preferred_element_type=F32)


def kernel(n, chunks, vid, own, hid, w_hbm, s_hbm, e_hbm, out, wbuf, sbuf, ebuf, hperm, snd, rcv,
           part, arcv, bsnd, brcv, keep, csnd, crcv, wsem, ssem, esem, dss, drs, asem, arem, bsem,
           brem, csem, crem, spread_out):
    me = lax.axis_index("tp")
    core, x, z = lax.rem(me, 2), lax.rem(me // 2, 2), me // 4
    nz = n // 4
    rows, cols = hid.shape
    per = rows // n
    group = nz * per
    half = cols // 2
    wide = wbuf.shape[2]
    folds = 16 // per
    narrow = wide // folds

    def load_w(c):
        at = pl.ds(pl.multiple_of(c * wide, wide), wide)
        return pltpu.make_async_copy(w_hbm.at[:, at], wbuf.at[c], wsem.at[c])

    load_s = pltpu.make_async_copy(s_hbm.at[0], sbuf, ssem)
    load_e = pltpu.make_async_copy(e_hbm.at[0], ebuf, esem)
    for c in range(chunks):
        load_w(c).start()
    load_s.start()
    load_e.start()

    barrier = pltpu.get_barrier_semaphore()

    @pl.loop(1, n)
    def _(d):
        pl.semaphore_signal(barrier, inc=1, device_id={"tp": lax.rem(me + d, n)}, device_id_type=MESH)

    variants = own.shape[1]
    named = vid[...] == iota((variants, rows), 0)
    named = named.astype(F32).astype(BF16)
    holder = contract(own[...].astype(F32).astype(BF16), named, 1, 0)
    same = contract(named, named, 0, 0)
    earlier = iota((rows, rows), 0) < iota((rows, rows), 1)
    order = jnp.sum(jnp.where(earlier, same, 0.0), axis=0, keepdims=True)
    slot = holder * CAP + order
    place = (slot == iota((n * CAP, rows), 0).astype(F32)).astype(F32).astype(BF16)
    halves = [
        contract(place, hid[:, h * half:(h + 1) * half], 1, 0).reshape(n, CAP, half) for h in range(2)
    ]
    snd[...] = jnp.concatenate(halves, axis=1).astype(BF16)
    rcv[0] = snd[me]

    at = iota((rows, rows), 0)
    r = at & (per - 1)
    z_of = lax.shift_right_logical(at, log2(per)) & (nz - 1)
    x_of = lax.shift_right_logical(at, log2(group)) & 1
    core_of = lax.shift_right_logical(at, log2(group) + 1)
    reorder = (((z_of * 2 + x_of) * 2 + core_of) * per + r == iota((rows, rows), 1))
    reorder = reorder.astype(F32).astype(BF16)
    hperm[...] = contract(reorder, hid[...], 1, 0).astype(BF16)
    mine = (slot == (iota((CAP, rows), 0) + me * CAP).astype(F32)).astype(F32).astype(BF16)
    spread = contract(reorder, mine, 1, 1).astype(BF16)

    pl.semaphore_wait(barrier, n - 1)

    def dispatch(d):
        to = lax.rem(me + d, n)
        return pltpu.make_async_remote_copy(
            src_ref=snd.at[to], dst_ref=rcv.at[d], send_sem=dss.at[d], recv_sem=drs.at[d],
            device_id={"tp": to}, device_id_type=MESH)

    order_out = ((1, n // 4), (n // 2, n), (n // 4, n // 2))
    for first, last in order_out:
        @pl.loop(first, last)
        def _(d):
            dispatch(d).start()

    @pl.loop(0, chunks)
    def _(c):
        load_w(c).wait()
        total = jnp.dot(hperm[...], wbuf[c], preferred_element_type=F32)
        part[c] = total.reshape(2, 2, group, wide)

    load_s.wait()

    def shrink(d, totals):
        start = lax.rem(me - d + n, n) * cols
        got = rcv[d]
        first = sbuf[:, pl.ds(pl.multiple_of(start, half), half)]
        second = sbuf[:, pl.ds(pl.multiple_of(start + half, half), half)]
        return totals[0] + contract(got, first, 1, 1), totals[1] + contract(got, second, 1, 1)

    zero = jnp.zeros((2 * CAP, sbuf.shape[0]), F32)
    totals = shrink(0, (zero, zero))
    for first, last in order_out:
        @pl.loop(first, last)
        def _(d):
            dispatch(d).wait_recv()

        for d in range(first, last):
            totals = shrink(d, totals)
    top, low = totals
    shrunk = (top[:CAP] + low[CAP:]).astype(BF16)
    spread_out[...] = contract(spread, shrunk, 1, 0).astype(BF16).reshape(2, 2 * group, -1)
    load_e.wait()

    def add_delta(c, to):
        at = pl.ds(pl.multiple_of(c * wide, wide), wide)
        delta = jnp.dot(spread_out[to], ebuf[:, at], preferred_element_type=F32)
        part[c, to] = part[c, to] + delta.astype(BF16).astype(F32).reshape(2, group, wide)

    def to_core(c):
        return pltpu.make_async_remote_copy(
            src_ref=part.at[c, 1 - core], dst_ref=arcv.at[c], send_sem=asem.at[c],
            recv_sem=arem.at[c], device_id={"tp": me + 1 - 2 * core}, device_id_type=MESH)

    def to_x(c):
        return pltpu.make_async_remote_copy(
            src_ref=bsnd.at[c], dst_ref=brcv.at[c], send_sem=bsem.at[c], recv_sem=brem.at[c],
            device_id={"tp": me + 2 - 4 * x}, device_id_type=MESH)

    def to_z(c, d):
        to = lax.rem(z + d, nz)
        return pltpu.make_async_remote_copy(
            src_ref=csnd.at[c, to], dst_ref=crcv.at[c, d - 1], send_sem=csem.at[c, d - 1],
            recv_sem=crem.at[c, d - 1], device_id={"tp": me + (to - z) * 4}, device_id_type=MESH)

    @pl.loop(0, chunks)
    def _(c):
        add_delta(c, 1 - core)
        to_core(c).start()

    @pl.loop(0, chunks)
    def _(c):
        add_delta(c, core)
        to_core(c).wait_recv()
        away = part[c, core, 1 - x] + arcv[c, 1 - x]
        away = jnp.concatenate([away[:, :wide // 2], away[:, wide // 2:]], axis=0)
        bsnd[c] = away.astype(BF16)
        to_x(c).start()
        keep[c] = part[c, core, x] + arcv[c, x]

    size = folds * group
    at = iota((size, size), 0)
    r = at & (per - 1)
    fold = lax.shift_right_logical(at, log2(per)) & (folds - 1)
    z_of = lax.shift_right_logical(at, log2(per * folds))
    refold = ((fold * nz + z_of) * per + r == iota((size, size), 1)).astype(F32).astype(BF16)

    @pl.loop(0, chunks)
    def _(c):
        to_x(c).wait_recv()
        got = brcv[c].astype(F32)
        total = keep[c] + jnp.concatenate([got[:group], got[group:]], axis=1)
        folded = jnp.concatenate(
            [total[:, j * narrow:(j + 1) * narrow] for j in range(folds)], axis=0).astype(BF16)
        csnd[c] = contract(refold, folded, 1, 0).astype(BF16).reshape(nz, 16, narrow)
        for d in range(1, nz):
            to_z(c, d).start()

    @pl.loop(0, chunks)
    def _(c):
        total = csnd[c, z].astype(F32)
        for d in range(1, nz):
            to_z(c, d).wait_recv()
            total = total + crcv[c, d - 1].astype(F32)
        row = jnp.concatenate([total[j * per:(j + 1) * per] for j in range(folds)], axis=1)
        out[:, pl.ds(pl.multiple_of(c * wide, wide), wide)] = row.astype(BF16)

    @pl.loop(1, n)
    def _(d):
        dispatch(d).wait_send()

    @pl.loop(0, chunks)
    def _(c):
        to_core(c).wait_send()
        to_x(c).wait_send()
        for d in range(1, nz):
            to_z(c, d).wait_send()


def fits(n, rows, cols, width):
    per = rows // n
    return (n % 4 == 0 and n <= 256 and cols % 256 == 0 and width % 2048 == 0 and per in (1, 2, 4, 8, 16)
            and rows == n * per and (n // 4) * per == 8)


def fused(hidden, down_weight, shrink_factor, expand_factor, variant_ids, owner):
    n = lax.axis_size("tp")
    rows, cols = hidden.shape
    rank, depth = shrink_factor.shape[1:]
    width = down_weight.shape[1]
    wide = 2048
    chunks = width // wide
    nz = n // 4
    per = rows // n
    group = nz * per
    narrow = wide * per // 16
    vmem = pl.BlockSpec(memory_space=pltpu.VMEM)
    hbm = pl.BlockSpec(memory_space=pl.ANY)
    dma = pltpu.SemaphoreType.DMA
    return pl.pallas_call(
        functools.partial(kernel, n, chunks),
        out_shape=jax.ShapeDtypeStruct((per, width), BF16),
        in_specs=[vmem, vmem, vmem, hbm, hbm, hbm],
        out_specs=vmem,
        scratch_shapes=[
            pltpu.VMEM((chunks, cols, wide), BF16),
            pltpu.VMEM((rank, depth), BF16),
            pltpu.VMEM((rank, width), BF16),
            pltpu.VMEM((rows, cols), BF16),
            pltpu.VMEM((n, 2 * CAP, cols // 2), BF16),
            pltpu.VMEM((n, 2 * CAP, cols // 2), BF16),
            pltpu.VMEM((chunks, 2, 2, group, wide), F32),
            pltpu.VMEM((chunks, 2, group, wide), F32),
            pltpu.VMEM((chunks, 2 * group, wide // 2), BF16),
            pltpu.VMEM((chunks, 2 * group, wide // 2), BF16),
            pltpu.VMEM((chunks, group, wide), F32),
            pltpu.VMEM((chunks, nz, 16, narrow), BF16),
            pltpu.VMEM((chunks, nz - 1, 16, narrow), BF16),
            dma((chunks,)), dma(()), dma(()), dma((n,)), dma((n,)),
            dma((chunks,)), dma((chunks,)), dma((chunks,)), dma((chunks,)),
            dma((chunks, nz - 1)), dma((chunks, nz - 1)),
            pltpu.VMEM((2, 2 * group, rank), BF16),
        ],
        compiler_params=pltpu.CompilerParams(
            collective_id=0, has_side_effects=True, vmem_limit_bytes=56 * 2**20),
        name="fused",
    )(variant_ids.reshape(1, -1), owner.reshape(1, -1), hidden, down_weight, shrink_factor, expand_factor)


def general(hidden, down_weight, shrink_factor, expand_factor, variant_ids, owner):
    group_size = lax.axis_size("tp")
    my_index = lax.axis_index("tp")
    row_count = hidden.shape[0]
    col_count = hidden.shape[1]
    width_out = expand_factor.shape[2]
    rank_width = shrink_factor.shape[1]
    capacity = CAP
    variant_of = variant_ids[:, 0]
    holder = owner[variant_of]
    held_here = holder == my_index
    onehot = (variant_of[:, None] == jnp.arange(owner.shape[0], dtype=jnp.int32)[None, :]).astype(
        jnp.int32
    )
    earlier = jnp.cumsum(onehot, axis=0) - onehot
    order_in = jnp.sum(earlier * onehot, axis=1)
    request_index = jnp.arange(row_count, dtype=jnp.int32)
    slices = lax.all_to_all(shrink_factor, "tp", split_axis=2, concat_axis=0, tiled=True)
    all_rows = slices.reshape(group_size * rank_width, col_count)
    every_slot = lax.dot_general(
        hidden, all_rows, (((1,), (1,)), ((), ())), preferred_element_type=jnp.float32
    )
    every_slot = every_slot.reshape(row_count, group_size, rank_width)
    chosen = holder[:, None] == jnp.arange(group_size, dtype=jnp.int32)[None, :]
    partial_value = jnp.sum(jnp.where(chosen[:, :, None], every_slot, jnp.float32(0.0)), axis=1)
    shrunk = lax.psum(partial_value, "tp").astype(jnp.bfloat16)
    source = jnp.full((capacity,), row_count, jnp.int32)
    source = source.at[jnp.where(held_here, order_in, capacity)].set(request_index, mode="drop")
    padded_shrunk = jnp.concatenate([shrunk, jnp.zeros((1, shrunk.shape[1]), jnp.bfloat16)], axis=0)
    delta_rows = jnp.dot(
        padded_shrunk[source], expand_factor[0], preferred_element_type=jnp.float32
    ).astype(jnp.bfloat16)
    delta_table = jnp.concatenate([delta_rows, jnp.zeros((1, width_out), jnp.bfloat16)], axis=0)
    pick_index = jnp.where(held_here, order_in, capacity)
    block_base = jnp.dot(hidden, down_weight, preferred_element_type=jnp.float32)
    summed = lax.psum_scatter(
        block_base + delta_table[pick_index].astype(jnp.float32),
        "tp",
        scatter_dimension=0,
        tiled=True,
    )
    return summed.astype(jnp.bfloat16)


def local(hidden, down_weight, shrink_factor, expand_factor, variant_ids, owner):
    n = lax.axis_size("tp")
    form = fused if fits(n, *hidden.shape, down_weight.shape[1]) else general
    return form(hidden, down_weight, shrink_factor, expand_factor, variant_ids, owner)


def solution(mesh):
    in_specs = (
        P("rep", "tp"),
        P("tp", None),
        P("tp", None, None),
        P("tp", None, None),
        P("rep", None),
        P(),
    )
    out_specs = P(("rep", "tp"), None)
    return jax.shard_map(local, mesh=mesh, in_specs=in_specs, out_specs=out_specs, check_vma=False)
```
